512 devices in a mesh: dp: 4 (over y_lo), seq: 64 (over x, z, core), tensor: 2 (over y_hi).
Axes of the slice: x: 4, y: 8 (y_hi: 2, y_lo: 4; y = y_hi * 4 + y_lo), z: 8, core: 2. Of those that a mesh axis runs over, the one named last changes fastest.
Arguments:
- img_query: bfloat16 [64, 512, 1280], P('seq', 'dp', 'tensor'), may hold values from -8 to 8
- img_key: bfloat16 [64, 512, 1280], P('seq', 'dp', 'tensor'), may hold values from -8 to 8
- img_value: bfloat16 [64, 512, 1280], P('seq', 'dp', 'tensor'), may hold values from -6 to 6
- txt_query: bfloat16 [64, 128, 1280], P('seq', None, 'tensor'), may hold values from -8 to 8
- txt_key: bfloat16 [64, 128, 1280], P('seq', None, 'tensor'), may hold values from -8 to 8
- txt_value: bfloat16 [64, 128, 1280], P('seq', None, 'tensor'), may hold values from -6 to 6
- img_cotangent: bfloat16 [64, 512, 1280], P('seq', 'dp', 'tensor'), may hold values from -6 to 6
- txt_cotangent: bfloat16 [64, 128, 1280], P('seq', None, 'tensor'), may hold values from -6 to 6
- norm_gains: float32 [4, 64], replicated, may hold values from 1 to 3
Outputs:
- img_out: bfloat16 [64, 512, 1280], P('seq', 'dp', 'tensor')
- txt_out: bfloat16 [64, 128, 1280], P('seq', None, 'tensor')
- img_grads: bfloat16 [3, 64, 512, 1280], P(None, 'seq', 'dp', 'tensor')
- txt_grads: bfloat16 [3, 64, 128, 1280], P(None, 'seq', None, 'tensor')
- gain_grads: float32 [4, 64], replicated
The draws below stay inside these ranges and needn't reach their ends.
All inputs are finite; a program needn't handle non-finite values.
Results may differ from the reference program's by a relative error of at most 0.02.
Values may be sent and summed in bfloat16 or wider, within the bound.
A program may use at most 64 MiB of HBM per device.

```python
import math
import jax
import jax.numpy as jnp
from jax import lax

HEADS = 20
HEAD_DIM = 64
TXT = 128
BATCH = 64
IMG = 512


def scaled_rows(key, row_count, lowest, highest):
    first_key, second_key = jax.random.split(key)
    entries = jax.random.normal(first_key, (BATCH, row_count, HEADS, HEAD_DIM), jnp.float32)
    scales = jnp.exp(jax.random.uniform(second_key, (BATCH, row_count, HEADS, 1), jnp.float32, lowest, highest))
    return jnp.clip(entries * scales, -8.0, 8.0).reshape(BATCH, row_count, HEADS * HEAD_DIM).astype(jnp.bfloat16)


def draw_img_query(key, part):
    key = jax.random.fold_in(key, 11)
    return scaled_rows(key, IMG, -1.2, 1.2)


def draw_img_key(key, part):
    key = jax.random.fold_in(key, 12)
    return scaled_rows(key, IMG, -1.2, 1.2)


def draw_txt_query(key, part):
    key = jax.random.fold_in(key, 13)
    return scaled_rows(key, TXT, -1.2, 1.2)


def draw_txt_key(key, part):
    key = jax.random.fold_in(key, 14)
    return scaled_rows(key, TXT, -1.2, 1.2)


def block_levels(stream_key, shape, shards, low, top_value):
    factor_of, own = 1.0, jax.random.fold_in(stream_key, 6)
    for dim, blocks in shards:
        steps = jnp.exp(jax.random.uniform(jax.random.fold_in(own, dim), (blocks,), jnp.float32, low / len(shards), top_value / len(shards)))
        factor_of = factor_of * jnp.repeat(steps, shape[dim] // blocks).reshape([-1 if axis == dim else 1 for axis in range(len(shape))])
    return factor_of


def gaussian(stream_key, dims, scale, reach, pieces=(), held_as=jnp.bfloat16):
    factor_of = block_levels(stream_key, dims, pieces, -0.22, 0.18) if pieces else 1.0
    drawn = jax.random.normal(stream_key, dims, jnp.float32) * scale * factor_of
    return jnp.minimum(jnp.maximum(drawn, -reach), reach).astype(held_as)


def setup_inputs(seed: int = 0) -> dict:
    splits = jax.random.split(jax.random.key(seed), 10)
    img_query = draw_img_query(jax.random.fold_in(splits[9], 71), 0)
    img_key = draw_img_key(jax.random.fold_in(splits[9], 71), 0)
    img_value = gaussian(splits[2], (BATCH, IMG, HEADS * HEAD_DIM), 1.0, 6.0, ((0, 64), (1, 4), (2, 2)))
    txt_query = draw_txt_query(jax.random.fold_in(splits[9], 71), 0)
    txt_key = draw_txt_key(jax.random.fold_in(splits[9], 71), 0)
    txt_value = gaussian(splits[5], (BATCH, TXT, HEADS * HEAD_DIM), 1.0, 6.0, ((0, 64), (2, 2)))
    img_cotangent = gaussian(splits[6], (BATCH, IMG, HEADS * HEAD_DIM), 1.0, 6.0, ((0, 64), (1, 4), (2, 2)))
    txt_cotangent = gaussian(splits[7], (BATCH, TXT, HEADS * HEAD_DIM), 1.0, 6.0, ((0, 64), (2, 2)))
    norm_gains = jnp.clip(jnp.exp(jax.random.uniform(splits[8], (4, HEAD_DIM), jnp.float32, math.log(1.0), math.log(3.0))), 1.0, 3.0)
    return {"img_query": img_query, "img_key": img_key, "img_value": img_value, "txt_query": txt_query, "txt_key": txt_key, "txt_value": txt_value, "img_cotangent": img_cotangent, "txt_cotangent": txt_cotangent, "norm_gains": norm_gains}


epsilon = 1e-06

def norm_forward(values, gain_row):
    inverse = lax.rsqrt(lax.optimization_barrier(jnp.mean(values * values, axis=-1, keepdims=True)) + epsilon)
    unit_rows = values * inverse
    return (unit_rows, inverse, (unit_rows * gain_row).astype(jnp.bfloat16))

def norm_backward(gradient, unit_rows, inverse, gain_row):
    weighted = gradient * gain_row
    inner = lax.optimization_barrier(jnp.mean(weighted * unit_rows, axis=-1, keepdims=True))
    result = (inverse * (weighted - unit_rows * inner)).astype(jnp.bfloat16)
    return (result, lax.optimization_barrier(jnp.sum(gradient * unit_rows, axis=(0, 1, 2))))

def head_pass(operands):
    queries, keys_in, values_in, cotangent = operands
    factor = HEAD_DIM ** (-0.5)
    scores = jnp.dot(queries, keys_in.T, preferred_element_type=jnp.float32) * factor
    exponent = jnp.exp(scores)
    totals = lax.optimization_barrier(jnp.sum(exponent, axis=-1))
    numerator = jnp.dot(exponent.astype(jnp.bfloat16), values_in, preferred_element_type=jnp.float32)
    output = (numerator / totals[:, None]).astype(jnp.bfloat16)
    logtotal = jnp.log(totals)
    probability = jnp.exp(scores - logtotal[:, None])
    deltas = lax.optimization_barrier(jnp.sum(cotangent.astype(jnp.float32) * output.astype(jnp.float32), axis=-1))
    grad_prob = jnp.dot(cotangent, values_in.T, preferred_element_type=jnp.float32)
    grad_score = (probability * (grad_prob - deltas[:, None])).astype(jnp.bfloat16)
    grad_value = jnp.dot(probability.astype(jnp.bfloat16).T, cotangent, preferred_element_type=jnp.float32)
    grad_query = jnp.dot(grad_score, keys_in, preferred_element_type=jnp.float32) * factor
    grad_key = jnp.dot(grad_score.T, queries, preferred_element_type=jnp.float32) * factor
    return (output, grad_query, grad_key, grad_value)

def split_heads(array):
    return array.reshape(array.shape[0], array.shape[1], HEADS, HEAD_DIM)

def to_items(array):
    return jnp.transpose(array, (0, 2, 1, 3)).reshape(BATCH * HEADS, array.shape[1], HEAD_DIM)

def from_items(array):
    return jnp.transpose(array.reshape(BATCH, HEADS, array.shape[1], HEAD_DIM), (0, 2, 1, 3))

def reference(img_query, img_key, img_value, txt_query, txt_key, txt_value, img_cotangent, txt_cotangent, norm_gains):
    unit_iq, inv_iq, normed_iq = norm_forward(split_heads(img_query).astype(jnp.float32), norm_gains[0])
    unit_ik, inv_ik, normed_ik = norm_forward(split_heads(img_key).astype(jnp.float32), norm_gains[1])
    unit_tq, inv_tq, normed_tq = norm_forward(split_heads(txt_query).astype(jnp.float32), norm_gains[2])
    unit_tk, inv_tk, normed_tk = norm_forward(split_heads(txt_key).astype(jnp.float32), norm_gains[3])
    joint_q = jnp.concatenate([normed_iq, normed_tq], axis=1)
    joint_k = jnp.concatenate([normed_ik, normed_tk], axis=1)
    joint_v = jnp.concatenate([split_heads(img_value), split_heads(txt_value)], axis=1)
    joint_g = jnp.concatenate([split_heads(img_cotangent), split_heads(txt_cotangent)], axis=1)
    results = lax.map(head_pass, (to_items(joint_q), to_items(joint_k), to_items(joint_v), to_items(joint_g)))
    output = from_items(results[0])
    grad_query = from_items(results[1])
    grad_key = from_items(results[2])
    grad_value = from_items(results[3])
    grad_iq, gain_iq = norm_backward(grad_query[:, :IMG], unit_iq, inv_iq, norm_gains[0])
    grad_tq, gain_tq = norm_backward(grad_query[:, IMG:], unit_tq, inv_tq, norm_gains[2])
    grad_ik, gain_ik = norm_backward(grad_key[:, :IMG], unit_ik, inv_ik, norm_gains[1])
    grad_tk, gain_tk = norm_backward(grad_key[:, IMG:], unit_tk, inv_tk, norm_gains[3])
    row_width = HEADS * HEAD_DIM
    img_out = output[:, :IMG].reshape(BATCH, IMG, row_width)
    txt_out = output[:, IMG:].reshape(BATCH, TXT, row_width)
    img_grads = jnp.stack([grad_iq.reshape(BATCH, IMG, row_width), grad_ik.reshape(BATCH, IMG, row_width), grad_value[:, :IMG].reshape(BATCH, IMG, row_width).astype(jnp.bfloat16)])
    txt_grads = jnp.stack([grad_tq.reshape(BATCH, TXT, row_width), grad_tk.reshape(BATCH, TXT, row_width), grad_value[:, IMG:].reshape(BATCH, TXT, row_width).astype(jnp.bfloat16)])
    gain_grads = jnp.stack([gain_iq, gain_ik, gain_tq, gain_tk])
    return (img_out, txt_out, img_grads, txt_grads, gain_grads)
```

```python
import jax
import jax.numpy as jnp
from jax import lax
from jax.experimental import pallas as pl
from jax.experimental.pallas import tpu as pltpu
from jax.sharding import PartitionSpec as P

HEAD_DIM = 64
EPSILON = 1e-6
ROWS = 128
LANES = 128
BLOCKS = 5
TEXT = 4 * ROWS
LOG2E = 1.4426950408889634
MESH = pl.DeviceIdType.MESH
NT = (((1,), (1,)), ((), ()))
f32, bf16 = jnp.float32, jnp.bfloat16


def dot(a, b):
    return jnp.dot(a, b, preferred_element_type=f32)


def dot_nt(a, b):
    return lax.dot_general(a, b, NT, preferred_element_type=f32)


def first_head():
    return lax.broadcasted_iota(jnp.int32, (ROWS, LANES), 1) < HEAD_DIM


def same_head():
    row = lax.broadcasted_iota(jnp.int32, (2 * LANES, LANES), 0)
    lane = lax.broadcasted_iota(jnp.int32, (2 * LANES, LANES), 1)
    return jnp.where(lax.rem(row, LANES) // HEAD_DIM == lane // HEAD_DIM, 1.0, 0.0).astype(bf16)


def identity():
    row = lax.broadcasted_iota(jnp.int32, (LANES, LANES), 0)
    lane = lax.broadcasted_iota(jnp.int32, (LANES, LANES), 1)
    return jnp.where(row == lane, 1.0, 0.0).astype(bf16)


def head_mean(z, same):
    high = z.astype(bf16)
    low = (z - high.astype(f32)).astype(bf16)
    return dot(jnp.concatenate([high, low], axis=1), same) * (1.0 / HEAD_DIM)


def norm(x, same):
    r = lax.rsqrt(head_mean(x * x, same) + EPSILON)
    return x * r, r


def norm_back(y, u, r, gain, same):
    w = y * gain
    return (r * (w - u * head_mean(w * u, same))).astype(bf16)


def by_head(x, first):
    zero = jnp.zeros_like(x)
    return jnp.concatenate([jnp.where(first, x, zero), jnp.where(first, zero, x)], axis=0)


def own_blocks(x):
    return jnp.concatenate([x[:HEAD_DIM, :ROWS], x[HEAD_DIM:, ROWS:]], axis=0)


def prepare_keys(rows, ins, gain, nk, uk, rk):
    u, r = norm(ins[1, rows, :].astype(f32), same_head())
    uk[rows, :] = u
    rk[rows, :] = r
    nk[rows, :] = (u * gain).astype(bf16)


def query_block(first_block, rows, ins, gain, nk, kt, vt, dk, dv, outs):
    same, first, eye = same_head(), first_head(), identity()
    u, r = norm(ins[0, rows, :].astype(f32), same)
    q = by_head((u * gain).astype(bf16), first)
    cot = ins[3, rows, :]
    g = by_head(cot, first)
    s = dot_nt(nk[...], q)
    e = jnp.exp2(s * (LOG2E * HEAD_DIM**-0.5))
    total = jnp.sum(e, axis=0, keepdims=True)
    p = e * (1.0 / total)
    pb = p.astype(bf16)
    out_t = own_blocks(dot(vt[...], pb)).astype(bf16)
    outs[0, rows, :] = dot_nt(eye, out_t).astype(bf16)
    z = out_t.astype(f32) * dot_nt(eye, cot)
    delta = jnp.concatenate(
        [
            jnp.sum(z[:HEAD_DIM], axis=0, keepdims=True),
            jnp.sum(z[HEAD_DIM:], axis=0, keepdims=True),
        ],
        axis=1,
    )
    ds = (p * (dot_nt(ins[2], g) - delta)).astype(bf16)
    new_dk, new_dv = dot(ds, q), dot(pb, g)
    if first_block:
        dk[...] = new_dk
        dv[...] = new_dv
    else:
        dk[...] += new_dk
        dv[...] += new_dv
    y = jnp.transpose(own_blocks(dot(kt[...], ds))) * HEAD_DIM**-0.5
    outs[1, rows, :] = norm_back(y, u, r, gain, same)
    return jnp.sum(y * u, axis=0, keepdims=True)


def key_block(rows, gain, dk, dv, uk, rk, outs):
    y = dk[rows, :] * HEAD_DIM**-0.5
    u, r = uk[rows, :], rk[rows, :]
    outs[2, rows, :] = norm_back(y, u, r, gain, same_head())
    outs[3, rows, :] = dv[rows, :].astype(bf16)
    return jnp.sum(y * u, axis=0, keepdims=True)


def kernel(
    iq, ik, iv, tq, tk, tv, ig, tg, gains_ref,
    img_out, txt_out, img_grads, txt_grads, gain_out,
    inb, outb, nk, uk, rk, kt, vt, dk, dv, gacc, racc, rbuf,
    in_local, in_send, in_recv, out_send, out_recv,
    txt_local, txt_send, txt_recv, gate_send, gate_recv, pass_send,
    red_send, red_recv,
):
    me = lax.axis_index("dp")
    seq = lax.axis_index("seq")
    tensor = lax.axis_index("tensor")
    core, z, x = lax.rem(seq, 2), lax.rem(seq // 2, 8), seq // 16
    y = tensor * 4 + me
    side = me // 2
    partner = me + 1 - 2 * lax.rem(me, 2)
    far_gate = 2 - side
    is_gate = jnp.logical_or(me == 1, me == 2)
    extra = 3 * core
    images = (iq, ik, iv, ig)
    texts = (tq, tk, tv, tg)

    def columns(owner):
        return pl.ds(pl.multiple_of(owner * LANES, LANES), LANES)

    def block(index):
        return pl.ds(pl.multiple_of(index * ROWS, ROWS), ROWS)

    def peer(i):
        return lax.rem(me + i, 4)

    def source(i):
        return lax.rem(me + 4 - i, 4)

    def dp(index):
        return (index, seq, tensor)

    def remote(src, dst, send, recv, to):
        return pltpu.make_async_remote_copy(
            src_ref=src, dst_ref=dst, send_sem=send, recv_sem=recv, device_id=to, device_id_type=MESH
        )

    def load(t, a, part):
        owner = me if t == 0 else 4
        src = (images if part == 0 else texts)[a].at[0, :, columns(owner)]
        rows = block(me) if part == 0 else pl.ds(TEXT, ROWS)
        return pltpu.make_async_copy(src, inb.at[t, a, rows], in_local.at[t, a, part])

    for a in (1, 2, 0, 3):
        for part in (1, 0):
            load(0, a, part).start()

    @pl.when(me == extra)
    def _():
        for a in (1, 2, 0, 3):
            for part in (1, 0):
                load(1, a, part).start()

    stages = (
        [
            (me, (lax.rem(x + i, 4) * 8 + z) * 2 + lax.rem(core + j, 2), tensor)
            for i in range(4)
            for j in range(2)
            if i or j
        ],
        [(me, (x * 8 + lax.rem(z + i, 8)) * 2 + core, tensor) for i in range(1, 8)],
        [(lax.rem(y + i, 4), seq, lax.rem(y + i, 8) // 4) for i in range(1, 8)],
    )

    barrier = pltpu.get_barrier_semaphore()
    for stage in stages:
        for to in stage:
            pl.semaphore_signal(barrier, inc=1, device_id=to, device_id_type=MESH)
    pl.semaphore_wait(barrier, sum(len(stage) for stage in stages))

    def hand(a, i):
        to = peer(i)
        return remote(
            images[a].at[0, :, columns(to)], inb.at[0, a, block(me)],
            in_send.at[0, a, i], in_recv.at[0, a, i], dp(to),
        )

    extra_way = lax.rem(extra + 4 - me, 4)

    def hand_extra(a):
        return remote(
            images[a].at[0, :, columns(4)], inb.at[1, a, block(me)],
            in_send.at[1, a, 0], in_recv.at[1, a, extra_way], dp(extra),
        )

    for pair in ((1, 2), (0, 3)):
        for i in (2, 3, 1):
            for a in pair:
                hand(a, i).start()

    @pl.when(me != extra)
    def _():
        for a in (1, 2, 0, 3):
            hand_extra(a).start()

    def await_rows(t, a, j):
        if j == 0 or j == 1:
            part = 1 - j
            rows = pl.ds(TEXT, ROWS) if j == 0 else block(me)
            pltpu.make_async_copy(
                texts[a].at[0, :, columns(0)], inb.at[t, a, rows], in_local.at[t, a, part]
            ).wait()
        else:
            i = j - 1
            rows = inb.at[t, a, block(source(i))]
            remote(rows, rows, in_send.at[t, a, i], in_recv.at[t, a, i], dp(source(i))).wait_recv()

    def result(t, group, rows):
        return outb.at[t, pl.ds(2, 2), rows] if group == 2 else outb.at[t, group, rows]

    def place(refs, group, owner):
        if group == 0:
            return refs[0].at[0, :, columns(owner)]
        if group == 1:
            return refs[1].at[0, 0, :, columns(owner)]
        return refs[1].at[pl.ds(1, 2), 0, :, columns(owner)]

    img_refs, txt_refs = (img_out, img_grads), (txt_out, txt_grads)

    def owner_of(t):
        return jnp.where(t == 0, me, 4)

    def keep(t, group):
        return pltpu.make_async_copy(
            result(t, group, block(me)), place(img_refs, group, owner_of(t)), out_send.at[t, group, 0]
        )

    def give(t, group, i):
        to = peer(i)
        return remote(
            result(t, group, block(to)), place(img_refs, group, owner_of(t)),
            out_send.at[t, group, i], out_recv.at[t, group, i], dp(to),
        )

    def text_copies(t, group):
        rows = result(t, group, pl.ds(TEXT, ROWS))
        spot = place(txt_refs, group, owner_of(t))
        slot = jnp.where(t == 0, lax.rem(me, 2), 2)
        return (
            remote(rows, spot, gate_send.at[t, group], gate_recv.at[slot, group], dp(far_gate)),
            remote(rows, spot, txt_send.at[t, group], txt_recv.at[t, group], dp(partner)),
            pltpu.make_async_copy(rows, spot, txt_local.at[t, group]),
        )

    gain = [jnp.concatenate([gains_ref[k : k + 1, :]] * 2, axis=1) for k in range(4)]
    gacc[...] = jnp.zeros_like(gacc)

    def do_tile(t, carry):
        ins, outs = inb.at[t], outb.at[t]

        def rows_of(j):
            return pl.ds(TEXT, ROWS) if j == 0 else block(me) if j == 1 else block(source(j - 1))

        def send(j, group):
            if j == 0:
                for c in text_copies(t, group):
                    c.start()
            elif j == 1:
                keep(t, group).start()
            else:
                give(t, group, 5 - j).start()

        for j in range(BLOCKS):
            await_rows(t, 1, j)
            prepare_keys(rows_of(j), ins, gain[3 if j == 0 else 1], nk, uk, rk)
        for j in range(BLOCKS):
            await_rows(t, 2, j)
        eye = identity()
        kt[...] = dot_nt(eye, nk[...]).astype(bf16)
        vt[...] = dot_nt(eye, ins[2]).astype(bf16)
        parts = []
        for j in range(BLOCKS):
            await_rows(t, 0, j)
            await_rows(t, 3, j)
            parts.append(
                query_block(j == 0, rows_of(j), ins, gain[2 if j == 0 else 0], nk, kt, vt, dk, dv, outs)
            )
            send(j, 0)
            send(j, 1)
        key_parts = []
        for j in range(BLOCKS):
            key_parts.append(
                key_block(rows_of(j), gain[3 if j == 0 else 1], dk, dv, uk, rk, outs)
            )
            send(j, 2)
        gacc[...] += jnp.concatenate(
            [sum(parts[1:]), sum(key_parts[1:]), parts[0], key_parts[0]], axis=0
        )
        return carry

    lax.fori_loop(0, jnp.where(me == extra, 2, 1), do_tile, 0)

    def cross(slot, group):
        owner = (1 - side) * 2 + slot if slot < 2 else 4
        spot = place(txt_refs, group, owner)
        return remote(spot, spot, pass_send.at[slot, group], gate_recv.at[slot, group], dp(partner))

    def pass_on(slot):
        for group in range(3):
            cross(slot, group).wait_recv()

            @pl.when(is_gate)
            def _():
                cross(slot, group).start()

    lanes = gacc[...]
    racc[0] = lanes[:, :HEAD_DIM] + lanes[:, HEAD_DIM:]

    def exchange(n):
        return [
            remote(racc.at[n], rbuf.at[n, j], red_send.at[n, j], red_recv.at[n, j], to)
            for j, to in enumerate(stages[n])
        ]

    for n in range(3):
        for c in exchange(n):
            c.start()
        if n < 2:
            pass_on(n)
        else:

            @pl.when(extra // 2 != side)
            def _():
                pass_on(2)

        for c in exchange(n):
            c.wait()
        value = racc[n]
        for j in range(7):
            value = value + rbuf[n, j]
        if n < 2:
            racc[n + 1] = value
        else:
            gain_out[...] = value

    def finish(t):
        for group in range(3):
            keep(t, group).wait()
            for i in (1, 2, 3):
                give(t, group, i).wait_send()
            gate, near, here = text_copies(t, group)
            gate.wait_send()
            near.wait_send()
            here.wait()

    def await_partner(t, owner):
        for group in range(3):
            spot = place(txt_refs, group, owner)
            remote(spot, spot, txt_send.at[t, group], txt_recv.at[t, group], dp(partner)).wait_recv()

    def await_given(t, i, owner):
        for group in range(3):
            spot = place(img_refs, group, owner)
            remote(
                spot, spot, out_send.at[t, group, i], out_recv.at[t, group, i], dp(source(i))
            ).wait_recv()

    finish(0)
    await_partner(0, partner)
    for i in (1, 2, 3):
        await_given(0, i, source(i))
        for a in range(4):
            hand(a, i).wait_send()

    @pl.when(me == extra)
    def _():
        finish(1)

    @pl.when(me != extra)
    def _():
        await_given(1, lax.rem(me + 4 - extra, 4), 4)
        for a in range(4):
            hand_extra(a).wait_send()

    @pl.when(partner == extra)
    def _():
        await_partner(1, 4)

    @pl.when(is_gate)
    def _():
        for slot in (0, 1):
            for group in range(3):
                cross(slot, group).wait_send()

    @pl.when(jnp.logical_and(is_gate, extra // 2 != side))
    def _():
        for group in range(3):
            cross(2, group).wait_send()


def local(iq, ik, iv, tq, tk, tv, ig, tg, gains):
    rows, width = iq.shape[1], iq.shape[2]
    anywhere = pl.BlockSpec(memory_space=pl.ANY)
    vmem = pl.BlockSpec(memory_space=pltpu.VMEM)
    dma = pltpu.SemaphoreType.DMA
    out = jax.ShapeDtypeStruct((1, rows, width), bf16)
    grads = jax.ShapeDtypeStruct((3, 1, rows, width), bf16)
    tall = (BLOCKS * ROWS, LANES)
    wide = (LANES, BLOCKS * ROWS)
    return pl.pallas_call(
        kernel,
        out_shape=(out, out, grads, grads, jax.ShapeDtypeStruct(gains.shape, f32)),
        in_specs=[anywhere] * 8 + [vmem],
        out_specs=(anywhere,) * 4 + (vmem,),
        scratch_shapes=[
            pltpu.VMEM((2, 4, *tall), bf16),
            pltpu.VMEM((2, 4, *tall), bf16),
            pltpu.VMEM(tall, bf16),
            pltpu.VMEM(tall, f32),
            pltpu.VMEM(tall, f32),
            pltpu.VMEM(wide, bf16),
            pltpu.VMEM(wide, bf16),
            pltpu.VMEM(tall, f32),
            pltpu.VMEM(tall, f32),
            pltpu.VMEM((4, LANES), f32),
            pltpu.VMEM((3, 4, HEAD_DIM), f32),
            pltpu.VMEM((3, 7, 4, HEAD_DIM), f32),
            dma((2, 4, 2)),
            dma((2, 4, 4)),
            dma((2, 4, 4)),
            dma((2, 3, 4)),
            dma((2, 3, 4)),
            dma((2, 3)),
            dma((2, 3)),
            dma((2, 3)),
            dma((2, 3)),
            dma((3, 3)),
            dma((3, 3)),
            dma((3, 7)),
            dma((3, 7)),
        ],
        compiler_params=pltpu.CompilerParams(
            collective_id=0, has_side_effects=True, vmem_limit_bytes=48 << 20
        ),
        name="joint_attention",
    )(iq, ik, iv, tq, tk, tv, ig, tg, gains)


def solution(mesh):
    image, text = P("seq", "dp", "tensor"), P("seq", None, "tensor")
    in_specs = (image, image, image, text, text, text, image, text, P())
    out_specs = (image, text, P(None, "seq", "dp", "tensor"), P(None, "seq", None, "tensor"), P())
    return jax.shard_map(local, mesh=mesh, in_specs=in_specs, out_specs=out_specs, check_vma=False)
```

```python
import jax
import jax.numpy as jnp
from jax import lax
from jax.experimental import pallas as pl
from jax.experimental.pallas import tpu as pltpu
from jax.sharding import PartitionSpec as P

HEAD_DIM = 64
EPSILON = 1e-6
ROWS = 128
LANES = 128
BLOCKS = 5
TEXT = 4 * ROWS
LOG2E = 1.4426950408889634
MESH = pl.DeviceIdType.MESH
NT = (((1,), (1,)), ((), ()))
f32, bf16 = jnp.float32, jnp.bfloat16


def dot(a, b):
    return jnp.dot(a, b, preferred_element_type=f32)


def dot_nt(a, b):
    return lax.dot_general(a, b, NT, preferred_element_type=f32)


def first_head():
    return lax.broadcasted_iota(jnp.int32, (BLOCKS * ROWS, LANES), 1) < HEAD_DIM


def same_head():
    row = lax.broadcasted_iota(jnp.int32, (2 * LANES, LANES), 0)
    lane = lax.broadcasted_iota(jnp.int32, (2 * LANES, LANES), 1)
    return jnp.where(lax.rem(row, LANES) // HEAD_DIM == lane // HEAD_DIM, 1.0, 0.0).astype(bf16)


def identity():
    row = lax.broadcasted_iota(jnp.int32, (LANES, LANES), 0)
    lane = lax.broadcasted_iota(jnp.int32, (LANES, LANES), 1)
    return jnp.where(row == lane, 1.0, 0.0).astype(bf16)


def head_mean(z, same):
    high = z.astype(bf16)
    low = (z - high.astype(f32)).astype(bf16)
    return dot(jnp.concatenate([high, low], axis=1), same) * (1.0 / HEAD_DIM)


def norm(x, same):
    r = lax.rsqrt(head_mean(x * x, same) + EPSILON)
    return x * r, r


def norm_back(y, u, r, gain, same):
    w = y * gain
    return (r * (w - u * head_mean(w * u, same))).astype(bf16)


def by_head(x, first):
    zero = jnp.zeros_like(x)
    return jnp.concatenate([jnp.where(first, x, zero), jnp.where(first, zero, x)], axis=0)


def own_blocks(x):
    return jnp.concatenate([x[:HEAD_DIM, : BLOCKS * ROWS], x[HEAD_DIM:, BLOCKS * ROWS :]], axis=0)


def prepare_keys(ins, gain, nk, uk, rk, kt, vt):
    u, r = norm(ins[1].astype(f32), same_head())
    uk[...] = u
    rk[...] = r
    n = (u * gain).astype(bf16)
    nk[...] = n
    eye = identity()
    kt[...] = dot_nt(eye, n).astype(bf16)
    vt[...] = dot_nt(eye, ins[2]).astype(bf16)


def query_pass(ins, gain, nk, kt, vt, dk, dv, outs):
    same, first, eye = same_head(), first_head(), identity()
    u, r = norm(ins[0].astype(f32), same)
    q = by_head((u * gain).astype(bf16), first)
    cot = ins[3]
    g = by_head(cot, first)
    s = dot_nt(nk[...], q)
    e = jnp.exp2(s * (LOG2E * HEAD_DIM**-0.5))
    total = jnp.sum(e, axis=0, keepdims=True)
    p = e * (1.0 / total)
    pb = p.astype(bf16)
    out_t = own_blocks(dot(vt[...], pb)).astype(bf16)
    for b in range(BLOCKS):
        rows = slice(b * ROWS, (b + 1) * ROWS)
        outs[0, rows, :] = dot_nt(eye, out_t[:, rows]).astype(bf16)
    z = out_t.astype(f32) * dot_nt(eye, cot)
    delta = jnp.concatenate(
        [
            jnp.sum(z[:HEAD_DIM], axis=0, keepdims=True),
            jnp.sum(z[HEAD_DIM:], axis=0, keepdims=True),
        ],
        axis=1,
    )
    ds = (p * (dot_nt(ins[2], g) - delta)).astype(bf16)
    dk[...] = dot(ds, q)
    dv[...] = dot(pb, g)
    y = jnp.transpose(own_blocks(dot(kt[...], ds))) * HEAD_DIM**-0.5
    outs[1] = norm_back(y, u, r, gain, same)
    return y * u


def key_pass(gain, dk, dv, uk, rk, outs):
    y = dk[...] * HEAD_DIM**-0.5
    u, r = uk[...], rk[...]
    outs[2] = norm_back(y, u, r, gain, same_head())
    outs[3] = dv[...].astype(bf16)
    return y * u


def image_and_text(x):
    return [jnp.sum(x[:TEXT], axis=0, keepdims=True), jnp.sum(x[TEXT:], axis=0, keepdims=True)]


def kernel(
    iq, ik, iv, tq, tk, tv, ig, tg, gains_ref,
    img_out, txt_out, img_grads, txt_grads, gain_out,
    inb, outb, gain_rows, nk, uk, rk, kt, vt, dk, dv, gacc, racc, rbuf,
    in_local, in_send, in_recv, out_send, out_recv,
    txt_local, txt_send, txt_recv, gate_send, gate_recv, pass_send,
    red_send, red_recv, present,
):
    me = lax.axis_index("dp")
    seq = lax.axis_index("seq")
    tensor = lax.axis_index("tensor")
    core, z, x = lax.rem(seq, 2), lax.rem(seq // 2, 8), seq // 16
    y = tensor * 4 + me
    side = me // 2
    partner = me + 1 - 2 * lax.rem(me, 2)
    far_gate = 2 - side
    is_gate = jnp.logical_or(me == 1, me == 2)
    extra = 3 * core
    images = (iq, ik, iv, ig)
    texts = (tq, tk, tv, tg)

    def columns(owner):
        return pl.ds(pl.multiple_of(owner * LANES, LANES), LANES)

    def block(index):
        return pl.ds(pl.multiple_of(index * ROWS, ROWS), ROWS)

    def peer(i):
        return lax.rem(me + i, 4)

    def source(i):
        return lax.rem(me + 4 - i, 4)

    def dp(index):
        return (index, seq, tensor)

    def remote(src, dst, send, recv, to):
        return pltpu.make_async_remote_copy(
            src_ref=src, dst_ref=dst, send_sem=send, recv_sem=recv, device_id=to, device_id_type=MESH
        )

    def load(t, a, part):
        owner = me if t == 0 else 4
        src = (images if part == 0 else texts)[a].at[0, :, columns(owner)]
        rows = block(me) if part == 0 else pl.ds(TEXT, ROWS)
        return pltpu.make_async_copy(src, inb.at[t, a, rows], in_local.at[t, a, part])

    for a in (1, 2, 0, 3):
        for part in (1, 0):
            load(0, a, part).start()

    @pl.when(me == extra)
    def _():
        for a in (1, 2, 0, 3):
            for part in (1, 0):
                load(1, a, part).start()

    def along_y(k):
        return (lax.rem(k, 4), seq, k // 4)

    def along_x(k):
        return (me, (lax.rem(k, 4) * 8 + z) * 2 + k // 4, tensor)

    def along_z(k):
        return (me, (x * 8 + k) * 2 + core, tensor)

    place_x = core * 4 + x
    rings = ((y, along_y), (place_x, along_x), (z, along_z))
    later = (4 * (1 - tensor), 7 - place_x, 7 - z)
    barrier = pltpu.get_barrier_semaphore()

    def greet(sem, to):
        pl.semaphore_signal(sem, inc=1, device_id=to, device_id_type=MESH)

    for i in (1, 2, 3):
        greet(barrier, dp(peer(i)))

    def each_pair(act, want_later):
        @pl.when(tensor == (0 if want_later else 1))
        def _():
            for k in range(4):
                act(0, (k, seq, 1 - tensor))

        for n in (1, 2):
            mine, member = rings[n]
            for k in range(8):
                ahead = mine < k if want_later else mine > k

                @pl.when(ahead)
                def _():
                    act(n, member(k))

    each_pair(lambda n, to: greet(barrier, to), True)
    pl.semaphore_wait(barrier, 3 + 4 * tensor + place_x + z)

    def hand(a, i):
        to = peer(i)
        return remote(
            images[a].at[0, :, columns(to)], inb.at[0, a, block(me)],
            in_send.at[0, a, i], in_recv.at[0, a, i], dp(to),
        )

    extra_way = lax.rem(extra + 4 - me, 4)

    def hand_extra(a):
        return remote(
            images[a].at[0, :, columns(4)], inb.at[1, a, block(me)],
            in_send.at[1, a, 0], in_recv.at[1, a, extra_way], dp(extra),
        )

    for pair in ((1, 2), (0, 3)):
        for i in (2, 3, 1):
            for a in pair:
                hand(a, i).start()

    @pl.when(me != extra)
    def _():
        for a in (1, 2, 0, 3):
            hand_extra(a).start()

    each_pair(lambda n, to: greet(present.at[n], to), False)

    def await_rows(t, a, j):
        if j == 0 or j == 1:
            part = 1 - j
            rows = pl.ds(TEXT, ROWS) if j == 0 else block(me)
            pltpu.make_async_copy(
                texts[a].at[0, :, columns(0)], inb.at[t, a, rows], in_local.at[t, a, part]
            ).wait()
        else:
            i = j - 1
            rows = inb.at[t, a, block(source(i))]
            remote(rows, rows, in_send.at[t, a, i], in_recv.at[t, a, i], dp(source(i))).wait_recv()

    def result(t, group, rows):
        return outb.at[t, pl.ds(2, 2), rows] if group == 2 else outb.at[t, group, rows]

    def place(refs, group, owner):
        if group == 0:
            return refs[0].at[0, :, columns(owner)]
        if group == 1:
            return refs[1].at[0, 0, :, columns(owner)]
        return refs[1].at[pl.ds(1, 2), 0, :, columns(owner)]

    img_refs, txt_refs = (img_out, img_grads), (txt_out, txt_grads)

    def owner_of(t):
        return jnp.where(t == 0, me, 4)

    def keep(t, group):
        return pltpu.make_async_copy(
            result(t, group, block(me)), place(img_refs, group, owner_of(t)), out_send.at[t, group, 0]
        )

    def give(t, group, i):
        to = peer(i)
        return remote(
            result(t, group, block(to)), place(img_refs, group, owner_of(t)),
            out_send.at[t, group, i], out_recv.at[t, group, i], dp(to),
        )

    def text_copies(t, group):
        rows = result(t, group, pl.ds(TEXT, ROWS))
        spot = place(txt_refs, group, owner_of(t))
        slot = jnp.where(t == 0, lax.rem(me, 2), 2)
        return (
            remote(rows, spot, gate_send.at[t, group], gate_recv.at[slot, group], dp(far_gate)),
            remote(rows, spot, txt_send.at[t, group], txt_recv.at[t, group], dp(partner)),
            pltpu.make_async_copy(rows, spot, txt_local.at[t, group]),
        )

    def send_text(t):
        for group in range(3):
            for c in text_copies(t, group):
                c.start()

    def send_images(t):
        for group in range(3):
            for i in (2, 3, 1):
                give(t, group, i).start()
            keep(t, group).start()

    def exchange(n):
        mine, member = rings[n]
        return [
            remote(
                racc.at[n], rbuf.at[n, i], red_send.at[n, i], red_recv.at[n, i], member(lax.rem(mine + i, 8))
            )
            for i in range(1, 8)
        ]

    def start_exchange(n):
        @pl.when(later[n] > 0)
        def _():
            pl.semaphore_wait(present.at[n], later[n])

        for c in exchange(n):
            c.start()

    def start_sums():
        lanes = gacc[...]
        racc[0] = lanes[:, :HEAD_DIM] + lanes[:, HEAD_DIM:]
        start_exchange(0)

    pairs = jnp.concatenate([gains_ref[...]] * 2, axis=1)
    is_text = lax.broadcasted_iota(jnp.int32, (BLOCKS * ROWS, LANES), 0) >= TEXT
    for k in range(2):
        gain_rows[k] = jnp.where(is_text, pairs[k + 2 : k + 3], pairs[k : k + 1])
    gacc[...] = jnp.zeros_like(gacc)

    def do_tile(t, carry):
        ins, outs = inb.at[t], outb.at[t]

        for a in (1, 2):
            for j in range(BLOCKS):
                await_rows(t, a, j)
        prepare_keys(ins, gain_rows[1], nk, uk, rk, kt, vt)
        for a in (0, 3):
            for j in range(BLOCKS):
                await_rows(t, a, j)
        query = image_and_text(query_pass(ins, gain_rows[0], nk, kt, vt, dk, dv, outs))
        key = image_and_text(key_pass(gain_rows[1], dk, dv, uk, rk, outs))
        gacc[...] += jnp.concatenate([query[0], key[0], query[1], key[1]], axis=0)

        @pl.when(t == 0)
        def _():
            @pl.when(me != extra)
            def _():
                start_sums()

            send_text(0)

            @pl.when(me != extra)
            def _():
                send_images(0)

        @pl.when(t == 1)
        def _():
            start_sums()
            send_images(0)
            send_text(1)
            send_images(1)

        return carry

    lax.fori_loop(0, jnp.where(me == extra, 2, 1), do_tile, 0)

    def cross(slot, group):
        owner = (1 - side) * 2 + slot if slot < 2 else 4
        spot = place(txt_refs, group, owner)
        return remote(spot, spot, pass_send.at[slot, group], gate_recv.at[slot, group], dp(partner))

    def pass_on(slot):
        for group in range(3):
            cross(slot, group).wait_recv()

            @pl.when(is_gate)
            def _():
                cross(slot, group).start()

    for n in range(3):
        if n == 2:
            pass_on(0)
            pass_on(1)
        for c in exchange(n):
            c.wait()
        value = racc[n]
        for i in range(1, 8):
            value = value + rbuf[n, i]
        if n < 2:
            racc[n + 1] = value
            start_exchange(n + 1)
        else:
            gain_out[...] = value

    @pl.when(extra // 2 != side)
    def _():
        pass_on(2)

    def finish(t):
        for group in range(3):
            keep(t, group).wait()
            for i in (1, 2, 3):
                give(t, group, i).wait_send()
            gate, near, here = text_copies(t, group)
            gate.wait_send()
            near.wait_send()
            here.wait()

    def await_partner(t, owner):
        for group in range(3):
            spot = place(txt_refs, group, owner)
            remote(spot, spot, txt_send.at[t, group], txt_recv.at[t, group], dp(partner)).wait_recv()

    def await_given(t, i, owner):
        for group in range(3):
            spot = place(img_refs, group, owner)
            remote(
                spot, spot, out_send.at[t, group, i], out_recv.at[t, group, i], dp(source(i))
            ).wait_recv()

    finish(0)
    await_partner(0, partner)
    for i in (1, 2, 3):
        await_given(0, i, source(i))
        for a in range(4):
            hand(a, i).wait_send()

    @pl.when(me == extra)
    def _():
        finish(1)

    @pl.when(me != extra)
    def _():
        await_given(1, lax.rem(me + 4 - extra, 4), 4)
        for a in range(4):
            hand_extra(a).wait_send()

    @pl.when(partner == extra)
    def _():
        await_partner(1, 4)

    @pl.when(is_gate)
    def _():
        for slot in (0, 1):
            for group in range(3):
                cross(slot, group).wait_send()

    @pl.when(jnp.logical_and(is_gate, extra // 2 != side))
    def _():
        for group in range(3):
            cross(2, group).wait_send()


def store_kernel(a, b, c, d, e, oa, ob, oc, od, oe, sems):
    copies = [
        pltpu.make_async_copy(src, dst, sems.at[n])
        for n, (src, dst) in enumerate(((a, oa), (b, ob), (c, oc), (d, od), (e, oe)))
    ]
    for copy in copies:
        copy.start()
    for copy in copies:
        copy.wait()


def store(results):
    anywhere = pl.BlockSpec(memory_space=pl.ANY)
    return pl.pallas_call(
        store_kernel,
        out_shape=tuple(jax.ShapeDtypeStruct(r.shape, r.dtype) for r in results),
        in_specs=[pl.BlockSpec(memory_space=pltpu.VMEM)] * 5,
        out_specs=(anywhere,) * 5,
        scratch_shapes=[pltpu.SemaphoreType.DMA((5,))],
        name="store_results",
    )(*results)


def local(iq, ik, iv, tq, tk, tv, ig, tg, gains):
    rows, width = iq.shape[1], iq.shape[2]
    anywhere = pl.BlockSpec(memory_space=pltpu.HBM)
    vmem = pl.BlockSpec(memory_space=pltpu.VMEM)
    dma = pltpu.SemaphoreType.DMA
    out = jax.ShapeDtypeStruct((1, rows, width), bf16)
    grads = jax.ShapeDtypeStruct((3, 1, rows, width), bf16)
    tall = (BLOCKS * ROWS, LANES)
    wide = (LANES, BLOCKS * ROWS)
    return store(pl.pallas_call(
        kernel,
        out_shape=(out, out, grads, grads, jax.ShapeDtypeStruct(gains.shape, f32)),
        in_specs=[anywhere] * 8 + [vmem],
        out_specs=(vmem,) * 5,
        scratch_shapes=[
            pltpu.VMEM((2, 4, *tall), bf16),
            pltpu.VMEM((2, 4, *tall), bf16),
            pltpu.VMEM((2, *tall), f32),
            pltpu.VMEM(tall, bf16),
            pltpu.VMEM(tall, f32),
            pltpu.VMEM(tall, f32),
            pltpu.VMEM(wide, bf16),
            pltpu.VMEM(wide, bf16),
            pltpu.VMEM(tall, f32),
            pltpu.VMEM(tall, f32),
            pltpu.VMEM((4, LANES), f32),
            pltpu.VMEM((3, 4, HEAD_DIM), f32),
            pltpu.VMEM((3, 8, 4, HEAD_DIM), f32),
            dma((2, 4, 2)),
            dma((2, 4, 4)),
            dma((2, 4, 4)),
            dma((2, 3, 4)),
            dma((2, 3, 4)),
            dma((2, 3)),
            dma((2, 3)),
            dma((2, 3)),
            dma((2, 3)),
            dma((3, 3)),
            dma((3, 3)),
            dma((3, 8)),
            dma((3, 8)),
            pltpu.SemaphoreType.REGULAR((3,)),
        ],
        compiler_params=pltpu.CompilerParams(
            collective_id=0, has_side_effects=True, vmem_limit_bytes=63 << 20
        ),
        name="joint_attention",
    )(iq, ik, iv, tq, tk, tv, ig, tg, gains))


def solution(mesh):
    image, text = P("seq", "dp", "tensor"), P("seq", None, "tensor")
    in_specs = (image, image, image, text, text, text, image, text, P())
    out_specs = (image, text, P(None, "seq", "dp", "tensor"), P(None, "seq", None, "tensor"), P())
    return jax.shard_map(local, mesh=mesh, in_specs=in_specs, out_specs=out_specs, check_vma=False)
```

```python
import jax
import jax.numpy as jnp
from jax import lax
from jax.experimental import pallas as pl
from jax.experimental.pallas import tpu as pltpu
from jax.sharding import PartitionSpec as P

HEAD_DIM = 64
EPSILON = 1e-6
ROWS = 128
LANES = 128
BLOCKS = 5
TEXT = 4 * ROWS
LOG2E = 1.4426950408889634
MESH = pl.DeviceIdType.MESH
NT = (((1,), (1,)), ((), ()))
f32, bf16 = jnp.float32, jnp.bfloat16


def dot(a, b):
    return jnp.dot(a, b, preferred_element_type=f32)


def dot_nt(a, b):
    return lax.dot_general(a, b, NT, preferred_element_type=f32)


def first_head():
    return lax.broadcasted_iota(jnp.int32, (BLOCKS * ROWS, LANES), 1) < HEAD_DIM


def same_head():
    row = lax.broadcasted_iota(jnp.int32, (2 * LANES, LANES), 0)
    lane = lax.broadcasted_iota(jnp.int32, (2 * LANES, LANES), 1)
    return jnp.where(lax.rem(row, LANES) // HEAD_DIM == lane // HEAD_DIM, 1.0, 0.0).astype(bf16)


def identity():
    row = lax.broadcasted_iota(jnp.int32, (LANES, LANES), 0)
    lane = lax.broadcasted_iota(jnp.int32, (LANES, LANES), 1)
    return jnp.where(row == lane, 1.0, 0.0).astype(bf16)


def head_mean(z, same):
    high = z.astype(bf16)
    low = (z - high.astype(f32)).astype(bf16)
    return dot(jnp.concatenate([high, low], axis=1), same) * (1.0 / HEAD_DIM)


def norm(x, same):
    r = lax.rsqrt(head_mean(x * x, same) + EPSILON)
    return x * r, r


def norm_back(y, u, r, gain, same):
    w = y * gain
    return (r * (w - u * head_mean(w * u, same))).astype(bf16)


def by_head(x, first):
    zero = jnp.zeros_like(x)
    return jnp.concatenate([jnp.where(first, x, zero), jnp.where(first, zero, x)], axis=0)


def own_blocks(x):
    return jnp.concatenate([x[:HEAD_DIM, : BLOCKS * ROWS], x[HEAD_DIM:, BLOCKS * ROWS :]], axis=0)


def prepare_keys(ins, gain, nk, uk, rk, kt, vt):
    u, r = norm(ins[0].astype(f32), same_head())
    uk[...] = u
    rk[...] = r
    n = (u * gain).astype(bf16)
    nk[...] = n
    eye = identity()
    kt[...] = dot_nt(eye, n).astype(bf16)
    vt[...] = dot_nt(eye, ins[1]).astype(bf16)


def query_pass(ins, gain, nk, kt, vt, dk, dv, outs):
    same, first, eye = same_head(), first_head(), identity()
    u, r = norm(ins[2].astype(f32), same)
    q = by_head((u * gain).astype(bf16), first)
    cot = ins[3]
    g = by_head(cot, first)
    s = dot_nt(nk[...], q)
    e = jnp.exp2(s * (LOG2E * HEAD_DIM**-0.5))
    total = jnp.sum(e, axis=0, keepdims=True)
    p = e * (1.0 / total)
    pb = p.astype(bf16)
    out_t = own_blocks(dot(vt[...], pb)).astype(bf16)
    for b in range(BLOCKS):
        rows = slice(b * ROWS, (b + 1) * ROWS)
        outs[0, rows, :] = dot_nt(eye, out_t[:, rows]).astype(bf16)
    z = out_t.astype(f32) * dot_nt(eye, cot)
    delta = jnp.concatenate(
        [
            jnp.sum(z[:HEAD_DIM], axis=0, keepdims=True),
            jnp.sum(z[HEAD_DIM:], axis=0, keepdims=True),
        ],
        axis=1,
    )
    ds = (p * (dot_nt(ins[1], g) - delta)).astype(bf16)
    dk[...] = dot(ds, q)
    dv[...] = dot(pb, g)
    y = jnp.transpose(own_blocks(dot(kt[...], ds))) * HEAD_DIM**-0.5
    outs[1] = norm_back(y, u, r, gain, same)
    return y * u


def key_pass(gain, dk, dv, uk, rk, outs):
    y = dk[...] * HEAD_DIM**-0.5
    u, r = uk[...], rk[...]
    outs[2] = norm_back(y, u, r, gain, same_head())
    outs[3] = dv[...].astype(bf16)
    return y * u


def image_and_text(x):
    return [jnp.sum(x[:TEXT], axis=0, keepdims=True), jnp.sum(x[TEXT:], axis=0, keepdims=True)]


def kernel(
    iq, ik, iv, tq, tk, tv, ig, tg, gains_ref,
    img_out, txt_out, img_grads, txt_grads, gain_out,
    inb, outb, gain_rows, nk, uk, rk, kt, vt, dk, dv, racc, rbuf,
    in_send, in_recv, kept, text_send, out_recv, cross_recv, pass_send, red_send, red_recv, present,
):
    me = lax.axis_index("dp")
    seq = lax.axis_index("seq")
    tensor = lax.axis_index("tensor")
    core, z, x = lax.rem(seq, 2), lax.rem(seq // 2, 8), seq // 16
    y = tensor * 4 + me
    side = me // 2
    partner = me + 1 - 2 * lax.rem(me, 2)
    far_gate = 2 - side
    is_gate = jnp.logical_or(me == 1, me == 2)
    extra = 3 * core
    images = (ik, iv, iq, ig)
    texts = (tk, tv, tq, tg)

    def columns(owner):
        return pl.ds(pl.multiple_of(owner * LANES, LANES), LANES)

    def block(index):
        return pl.ds(pl.multiple_of(index * ROWS, ROWS), ROWS)

    def peer(i):
        return lax.rem(me + i, 4)

    def dp(index):
        return (index, seq, tensor)

    def remote(src, dst, send, recv, to):
        return pltpu.make_async_remote_copy(
            src_ref=src, dst_ref=dst, send_sem=send, recv_sem=recv, device_id=to, device_id_type=MESH
        )

    def drain(like, sem):
        pltpu.make_async_copy(like, like, sem).wait()

    def load(t):
        owner = me if t == 0 else 4
        for a in range(4):
            for refs, rows in ((texts, pl.ds(TEXT, ROWS)), (images, block(me))):
                pltpu.make_async_copy(
                    refs[a].at[0, :, columns(owner)], inb.at[t, a, rows], in_recv.at[t, a // 2]
                ).start()

    def along_y(k):
        return (lax.rem(k, 4), seq, k // 4)

    def along_x(k):
        return (me, (lax.rem(k, 4) * 8 + z) * 2 + k // 4, tensor)

    def along_z(k):
        return (me, (x * 8 + k) * 2 + core, tensor)

    place_x = core * 4 + x
    rings = ((y, along_y), (place_x, along_x), (z, along_z))
    later = (4 * (1 - tensor), 7 - place_x, 7 - z)
    barrier = pltpu.get_barrier_semaphore()

    def greet(sem, to):
        pl.semaphore_signal(sem, inc=1, device_id=to, device_id_type=MESH)

    for i in (1, 2, 3):
        greet(barrier, dp(peer(i)))

    def each_pair(act, want_later):
        @pl.when(tensor == (0 if want_later else 1))
        def _():
            for k in range(4):
                act(0, (k, seq, 1 - tensor))

        for n in (1, 2):
            mine, member = rings[n]
            for k in range(8):
                ahead = mine < k if want_later else mine > k

                @pl.when(ahead)
                def _():
                    act(n, member(k))

    each_pair(lambda n, to: greet(barrier, to), True)
    load(0)

    @pl.when(me == extra)
    def _():
        load(1)

    pl.semaphore_wait(barrier, 3 + 4 * tensor + place_x + z)

    def hand(a, i):
        to = peer(i)
        remote(
            images[a].at[0, :, columns(to)], inb.at[0, a, block(me)],
            in_send.at[0], in_recv.at[0, a // 2], dp(to),
        ).start()

    for pair in ((0, 1), (2, 3)):
        for i in (2, 3, 1):
            for a in pair:
                hand(a, i)

    @pl.when(me != extra)
    def _():
        for a in range(4):
            remote(
                images[a].at[0, :, columns(4)], inb.at[1, a, block(me)],
                in_send.at[1], in_recv.at[1, a // 2], dp(extra),
            ).start()

    each_pair(lambda n, to: greet(present.at[n], to), False)

    def result(t, group, rows):
        return outb.at[t, pl.ds(2, 2), rows] if group == 2 else outb.at[t, group, rows]

    def place(refs, group, owner):
        if group == 0:
            return refs[0].at[0, :, columns(owner)]
        if group == 1:
            return refs[1].at[0, 0, :, columns(owner)]
        return refs[1].at[pl.ds(1, 2), 0, :, columns(owner)]

    img_refs, txt_refs = (img_out, img_grads), (txt_out, txt_grads)

    def owner_of(t):
        return jnp.where(t == 0, me, 4)

    def send_text(t):
        for group in range(3):
            rows = result(t, group, pl.ds(TEXT, ROWS))
            spot = place(txt_refs, group, owner_of(t))
            remote(rows, spot, text_send.at[t], cross_recv.at[t], dp(far_gate)).start()
            remote(rows, spot, text_send.at[t], out_recv.at[2 * t], dp(partner)).start()
            pltpu.make_async_copy(rows, spot, kept.at[t]).start()

    def send_images(t):
        for group in range(3):
            spot = place(img_refs, group, owner_of(t))
            for i in (2, 3, 1):
                to = peer(i)
                remote(result(t, group, block(to)), spot, kept.at[t], out_recv.at[t], dp(to)).start()
            pltpu.make_async_copy(result(t, group, block(me)), spot, kept.at[t]).start()

    def start_exchange(n):
        @pl.when(later[n] > 0)
        def _():
            pl.semaphore_wait(present.at[n], later[n])

        mine, member = rings[n]
        for i in range(1, 8):
            remote(
                racc.at[n], rbuf.at[n, i], red_send.at[n], red_recv.at[n], member(lax.rem(mine + i, 8))
            ).start()

    pairs = jnp.concatenate([gains_ref[...]] * 2, axis=1)
    is_text = lax.broadcasted_iota(jnp.int32, (BLOCKS * ROWS, LANES), 0) >= TEXT
    for k in range(2):
        gain_rows[k] = jnp.where(is_text, pairs[k + 2 : k + 3], pairs[k : k + 1])
    racc[0] = jnp.zeros((4, LANES), f32)

    def do_tile(t, carry):
        ins, outs = inb.at[t], outb.at[t]
        drain(inb.at[t, pl.ds(0, 2)], in_recv.at[t, 0])
        prepare_keys(ins, gain_rows[1], nk, uk, rk, kt, vt)
        drain(inb.at[t, pl.ds(2, 2)], in_recv.at[t, 1])
        query = image_and_text(query_pass(ins, gain_rows[0], nk, kt, vt, dk, dv, outs))
        key = image_and_text(key_pass(gain_rows[1], dk, dv, uk, rk, outs))
        racc[0] += jnp.concatenate([query[0], key[0], query[1], key[1]], axis=0)

        @pl.when(t == 0)
        def _():
            @pl.when(me != extra)
            def _():
                start_exchange(0)

            send_text(0)

            @pl.when(me != extra)
            def _():
                send_images(0)

        @pl.when(t == 1)
        def _():
            start_exchange(0)
            send_images(0)
            send_text(1)
            send_images(1)

        return carry

    lax.fori_loop(0, jnp.where(me == extra, 2, 1), do_tile, 0)

    def pass_on(t):
        owners = [4] if t else [(1 - side) * 2, (1 - side) * 2 + 1]
        drain(outb.at[t, :, pl.ds(0, ROWS * len(owners))], cross_recv.at[t])

        @pl.when(is_gate)
        def _():
            for group in range(3):
                for owner in owners:
                    spot = place(txt_refs, group, owner)
                    remote(spot, spot, pass_send.at[t], cross_recv.at[t], dp(partner)).start()

    for n in range(3):
        if n == 2:
            pass_on(0)
        drain(rbuf.at[n, pl.ds(1, 7)], red_send.at[n])
        drain(rbuf.at[n, pl.ds(1, 7)], red_recv.at[n])
        value = racc[n]
        for i in range(1, 8):
            value = value + rbuf[n, i]
        if n < 2:
            racc[n + 1] = value
            start_exchange(n + 1)
        else:
            gain_out[...] = value[:, :HEAD_DIM] + value[:, HEAD_DIM:]

    @pl.when(extra // 2 != side)
    def _():
        pass_on(1)

    def finish(t):
        drain(outb.at[t], kept.at[t])
        drain(outb.at[t, :, pl.ds(0, 2 * ROWS)], text_send.at[t])

    finish(0)
    drain(outb.at[0, :, pl.ds(0, 4 * ROWS)], out_recv.at[0])
    drain(inb.at[0, :, pl.ds(0, 3 * ROWS)], in_send.at[0])

    @pl.when(me == extra)
    def _():
        finish(1)

    @pl.when(me != extra)
    def _():
        drain(outb.at[0, :, pl.ds(0, ROWS)], out_recv.at[1])
        drain(inb.at[0, :, pl.ds(0, ROWS)], in_send.at[1])

    @pl.when(partner == extra)
    def _():
        drain(outb.at[0, :, pl.ds(0, ROWS)], out_recv.at[2])

    @pl.when(is_gate)
    def _():
        drain(outb.at[0, :, pl.ds(0, 2 * ROWS)], pass_send.at[0])

    @pl.when(jnp.logical_and(is_gate, extra // 2 != side))
    def _():
        drain(outb.at[0, :, pl.ds(0, ROWS)], pass_send.at[1])


def store_kernel(a, b, c, d, e, oa, ob, oc, od, oe, sems):
    copies = [
        pltpu.make_async_copy(src, dst, sems.at[n])
        for n, (src, dst) in enumerate(((a, oa), (b, ob), (c, oc), (d, od), (e, oe)))
    ]
    for copy in copies:
        copy.start()
    for copy in copies:
        copy.wait()


def store(results):
    anywhere = pl.BlockSpec(memory_space=pl.ANY)
    return pl.pallas_call(
        store_kernel,
        out_shape=tuple(jax.ShapeDtypeStruct(r.shape, r.dtype) for r in results),
        in_specs=[pl.BlockSpec(memory_space=pltpu.VMEM)] * 5,
        out_specs=(anywhere,) * 5,
        scratch_shapes=[pltpu.SemaphoreType.DMA((5,))],
        name="store_results",
    )(*results)


def local(iq, ik, iv, tq, tk, tv, ig, tg, gains):
    rows, width = iq.shape[1], iq.shape[2]
    anywhere = pl.BlockSpec(memory_space=pltpu.HBM)
    vmem = pl.BlockSpec(memory_space=pltpu.VMEM)
    dma = pltpu.SemaphoreType.DMA
    out = jax.ShapeDtypeStruct((1, rows, width), bf16)
    grads = jax.ShapeDtypeStruct((3, 1, rows, width), bf16)
    tall = (BLOCKS * ROWS, LANES)
    wide = (LANES, BLOCKS * ROWS)
    return store(pl.pallas_call(
        kernel,
        out_shape=(out, out, grads, grads, jax.ShapeDtypeStruct(gains.shape, f32)),
        in_specs=[anywhere] * 8 + [vmem],
        out_specs=(vmem,) * 5,
        scratch_shapes=[
            pltpu.VMEM((2, 4, *tall), bf16),
            pltpu.VMEM((2, 4, *tall), bf16),
            pltpu.VMEM((2, *tall), f32),
            pltpu.VMEM(tall, bf16),
            pltpu.VMEM(tall, f32),
            pltpu.VMEM(tall, f32),
            pltpu.VMEM(wide, bf16),
            pltpu.VMEM(wide, bf16),
            pltpu.VMEM(tall, f32),
            pltpu.VMEM(tall, f32),
            pltpu.VMEM((3, 4, LANES), f32),
            pltpu.VMEM((3, 8, 4, LANES), f32),
            dma((2,)),
            dma((2, 2)),
            dma((2,)),
            dma((2,)),
            dma((3,)),
            dma((2,)),
            dma((2,)),
            dma((3,)),
            dma((3,)),
            pltpu.SemaphoreType.REGULAR((3,)),
        ],
        compiler_params=pltpu.CompilerParams(
            collective_id=0, has_side_effects=True, vmem_limit_bytes=63 << 20
        ),
        name="joint_attention",
    )(iq, ik, iv, tq, tk, tv, ig, tg, gains))


def solution(mesh):
    image, text = P("seq", "dp", "tensor"), P("seq", None, "tensor")
    in_specs = (image, image, image, text, text, text, image, text, P())
    out_specs = (image, text, P(None, "seq", "dp", "tensor"), P(None, "seq", None, "tensor"), P())
    return jax.shard_map(local, mesh=mesh, in_specs=in_specs, out_specs=out_specs, check_vma=False)
```

```python
import jax
import jax.numpy as jnp
from jax import lax
from jax.experimental import pallas as pl
from jax.experimental.pallas import tpu as pltpu
from jax.sharding import PartitionSpec as P

HEAD_DIM = 64
EPSILON = 1e-6
ROWS = 128
LANES = 128
BLOCKS = 5
TEXT = 4 * ROWS
LOG2E = 1.4426950408889634
MESH = pl.DeviceIdType.MESH
NT = (((1,), (1,)), ((), ()))
f32, bf16 = jnp.float32, jnp.bfloat16


def dot(a, b):
    return jnp.dot(a, b, preferred_element_type=f32)


def dot_nt(a, b):
    return lax.dot_general(a, b, NT, preferred_element_type=f32)


def first_head():
    return lax.broadcasted_iota(jnp.int32, (BLOCKS * ROWS, LANES), 1) < HEAD_DIM


def same_head():
    row = lax.broadcasted_iota(jnp.int32, (2 * LANES, LANES), 0)
    lane = lax.broadcasted_iota(jnp.int32, (2 * LANES, LANES), 1)
    return jnp.where(lax.rem(row, LANES) // HEAD_DIM == lane // HEAD_DIM, 1.0, 0.0).astype(bf16)


def identity():
    row = lax.broadcasted_iota(jnp.int32, (LANES, LANES), 0)
    lane = lax.broadcasted_iota(jnp.int32, (LANES, LANES), 1)
    return jnp.where(row == lane, 1.0, 0.0).astype(bf16)


def head_mean(z, same):
    high = z.astype(bf16)
    low = (z - high.astype(f32)).astype(bf16)
    return dot(jnp.concatenate([high, low], axis=1), same) * (1.0 / HEAD_DIM)


def norm(x, same):
    r = lax.rsqrt(head_mean(x * x, same) + EPSILON)
    return x * r, r


def norm_back(y, u, r, gain, same):
    w = y * gain
    return (r * (w - u * head_mean(w * u, same))).astype(bf16)


def by_head(x, first):
    zero = jnp.zeros_like(x)
    return jnp.concatenate([jnp.where(first, x, zero), jnp.where(first, zero, x)], axis=0)


def own_blocks(x):
    return jnp.concatenate([x[:HEAD_DIM, : BLOCKS * ROWS], x[HEAD_DIM:, BLOCKS * ROWS :]], axis=0)


def prepare_keys(ins, gain, nk, uk, rk, kt, vt):
    u, r = norm(ins[0].astype(f32), same_head())
    uk[...] = u
    rk[...] = r
    n = (u * gain).astype(bf16)
    nk[...] = n
    eye = identity()
    kt[...] = dot_nt(eye, n).astype(bf16)
    vt[...] = dot_nt(eye, ins[1]).astype(bf16)


def query_pass(ins, gain, nk, kt, vt, dk, dv, outs, send_output):
    same, first, eye = same_head(), first_head(), identity()
    u, r = norm(ins[2].astype(f32), same)
    q = by_head((u * gain).astype(bf16), first)
    cot = ins[3]
    g = by_head(cot, first)
    s = dot_nt(nk[...], q)
    e = jnp.exp2(s * (LOG2E * HEAD_DIM**-0.5))
    total = jnp.sum(e, axis=0, keepdims=True)
    p = e * (1.0 / total)
    pb = p.astype(bf16)
    out_t = own_blocks(dot(vt[...], pb)).astype(bf16)
    for b in range(BLOCKS):
        rows = slice(b * ROWS, (b + 1) * ROWS)
        outs[0, rows, :] = dot_nt(eye, out_t[:, rows]).astype(bf16)
    send_output()
    z = out_t.astype(f32) * dot_nt(eye, cot)
    delta = jnp.concatenate(
        [
            jnp.sum(z[:HEAD_DIM], axis=0, keepdims=True),
            jnp.sum(z[HEAD_DIM:], axis=0, keepdims=True),
        ],
        axis=1,
    )
    ds = (p * (dot_nt(ins[1], g) - delta)).astype(bf16)
    dk[...] = dot(ds, q)
    dv[...] = dot(pb, g)
    y = jnp.transpose(own_blocks(dot(kt[...], ds))) * HEAD_DIM**-0.5
    outs[1] = norm_back(y, u, r, gain, same)
    return y * u


def key_pass(gain, dk, dv, uk, rk, outs):
    y = dk[...] * HEAD_DIM**-0.5
    u, r = uk[...], rk[...]
    outs[2] = norm_back(y, u, r, gain, same_head())
    outs[3] = dv[...].astype(bf16)
    return y * u


def image_and_text(x):
    return [jnp.sum(x[:TEXT], axis=0, keepdims=True), jnp.sum(x[TEXT:], axis=0, keepdims=True)]


def kernel(
    iq, ik, iv, tq, tk, tv, ig, tg, gains_ref,
    img_out, txt_out, img_grads, txt_grads, gain_out,
    inb, outb, gain_rows, nk, uk, rk, kt, vt, dk, dv, racc, rbuf,
    in_send, in_recv, kept, text_send, out_recv, cross_recv, pass_send, red_send, red_recv, total_send, total_recv, present,
):
    me = lax.axis_index("dp")
    seq = lax.axis_index("seq")
    tensor = lax.axis_index("tensor")
    core, z, x = lax.rem(seq, 2), lax.rem(seq // 2, 8), seq // 16
    y = tensor * 4 + me
    side = me // 2
    partner = me + 1 - 2 * lax.rem(me, 2)
    far_gate = 2 - side
    is_gate = jnp.logical_or(me == 1, me == 2)
    extra = 3 * core
    images = (ik, iv, iq, ig)
    texts = (tk, tv, tq, tg)

    def columns(owner):
        return pl.ds(pl.multiple_of(owner * LANES, LANES), LANES)

    def block(index):
        return pl.ds(pl.multiple_of(index * ROWS, ROWS), ROWS)

    def peer(i):
        return lax.rem(me + i, 4)

    def dp(index):
        return (index, seq, tensor)

    def remote(src, dst, send, recv, to):
        return pltpu.make_async_remote_copy(
            src_ref=src, dst_ref=dst, send_sem=send, recv_sem=recv, device_id=to, device_id_type=MESH
        )

    def drain(like, sem):
        pltpu.make_async_copy(like, like, sem).wait()

    def load(t):
        owner = me if t == 0 else 4
        for a in range(4):
            for refs, rows in ((texts, pl.ds(TEXT, ROWS)), (images, block(me))):
                pltpu.make_async_copy(
                    refs[a].at[0, :, columns(owner)], inb.at[t, a, rows], in_recv.at[t, a // 2]
                ).start()

    def along_y(k):
        return (lax.rem(k, 4), seq, k // 4)

    def along_x(k):
        return (me, (lax.rem(k, 4) * 8 + z) * 2 + k // 4, tensor)

    def along_z(k):
        return (me, (x * 8 + k) * 2 + core, tensor)

    place_x = core * 4 + x
    rings = ((y, along_y), (place_x, along_x), (z, along_z))
    later = (4 * (1 - tensor), 7 - place_x, 7 - z)
    barrier = pltpu.get_barrier_semaphore()

    def greet(sem, to):
        pl.semaphore_signal(sem, inc=1, device_id=to, device_id_type=MESH)

    for i in (1, 2, 3):
        greet(barrier, dp(peer(i)))

    def each_pair(act, want_later):
        @pl.when(tensor == (0 if want_later else 1))
        def _():
            for k in range(4):
                act(0, (k, seq, 1 - tensor))

        @pl.when(jnp.logical_not(is_gate))
        def _():
            for n in (1, 2):
                mine, member = rings[n]
                for k in range(8):
                    ahead = mine < k if want_later else mine > k

                    @pl.when(ahead)
                    def _():
                        act(n, member(k))

    each_pair(lambda n, to: greet(barrier, to), True)
    load(0)

    @pl.when(me == extra)
    def _():
        load(1)

    pl.semaphore_wait(barrier, 3 + 4 * tensor + jnp.where(is_gate, 0, place_x + z))

    def hand(a, i):
        to = peer(i)
        remote(
            images[a].at[0, :, columns(to)], inb.at[0, a, block(me)],
            in_send.at[0], in_recv.at[0, a // 2], dp(to),
        ).start()

    for pair in ((0, 1), (2, 3)):
        for i in (2, 3, 1):
            for a in pair:
                hand(a, i)

    @pl.when(me != extra)
    def _():
        for a in range(4):
            remote(
                images[a].at[0, :, columns(4)], inb.at[1, a, block(me)],
                in_send.at[1], in_recv.at[1, a // 2], dp(extra),
            ).start()

    each_pair(lambda n, to: greet(present.at[n], to), False)

    def result(t, group, rows):
        return outb.at[t, pl.ds(2, 2), rows] if group == 2 else outb.at[t, group, rows]

    def place(refs, group, owner):
        if group == 0:
            return refs[0].at[0, :, columns(owner)]
        if group == 1:
            return refs[1].at[0, 0, :, columns(owner)]
        return refs[1].at[pl.ds(1, 2), 0, :, columns(owner)]

    img_refs, txt_refs = (img_out, img_grads), (txt_out, txt_grads)

    def owner_of(t):
        return jnp.where(t == 0, me, 4)

    def send_text(t, groups):
        for group in groups:
            rows = result(t, group, pl.ds(TEXT, ROWS))
            spot = place(txt_refs, group, owner_of(t))
            remote(rows, spot, text_send.at[t], cross_recv.at[t], dp(far_gate)).start()
            remote(rows, spot, text_send.at[t], out_recv.at[2 * t], dp(partner)).start()
            pltpu.make_async_copy(rows, spot, kept.at[t]).start()

    def send_images(t, groups):
        for group in groups:
            spot = place(img_refs, group, owner_of(t))
            for i in (2, 3, 1):
                to = peer(i)
                remote(result(t, group, block(to)), spot, kept.at[t], out_recv.at[t], dp(to)).start()
            pltpu.make_async_copy(result(t, group, block(me)), spot, kept.at[t]).start()

    def start_exchange(n):
        @pl.when(later[n] > 0)
        def _():
            pl.semaphore_wait(present.at[n], later[n])

        mine, member = rings[n]
        for i in range(1, 8):
            remote(
                racc.at[n], rbuf.at[n, i], red_send.at[n], red_recv.at[n], member(lax.rem(mine + i, 8))
            ).start()

    pairs = jnp.concatenate([gains_ref[...]] * 2, axis=1)
    is_text = lax.broadcasted_iota(jnp.int32, (BLOCKS * ROWS, LANES), 0) >= TEXT
    for k in range(2):
        gain_rows[k] = jnp.where(is_text, pairs[k + 2 : k + 3], pairs[k : k + 1])
    racc[0] = jnp.zeros((4, LANES), f32)

    def do_tile(t, carry):
        ins, outs = inb.at[t], outb.at[t]

        def send_output():
            @pl.when(jnp.logical_and(t == 0, me != extra))
            def _():
                send_text(0, (0,))

        drain(inb.at[t, pl.ds(0, 2)], in_recv.at[t, 0])
        prepare_keys(ins, gain_rows[1], nk, uk, rk, kt, vt)
        drain(inb.at[t, pl.ds(2, 2)], in_recv.at[t, 1])
        query = image_and_text(query_pass(ins, gain_rows[0], nk, kt, vt, dk, dv, outs, send_output))
        key = image_and_text(key_pass(gain_rows[1], dk, dv, uk, rk, outs))
        racc[0] += jnp.concatenate([query[0], key[0], query[1], key[1]], axis=0)

        @pl.when(t == 0)
        def _():
            @pl.when(me != extra)
            def _():
                start_exchange(0)

            @pl.when(me != extra)
            def _():
                send_text(0, (1, 2))
                send_images(0, (0, 1, 2))

        @pl.when(t == 1)
        def _():
            start_exchange(0)
            send_text(0, (0, 1, 2))
            send_text(1, (0, 1, 2))
            send_images(0, (0, 1, 2))
            send_images(1, (0, 1, 2))

        return carry

    lax.fori_loop(0, jnp.where(me == extra, 2, 1), do_tile, 0)

    def pass_on(t):
        owners = [4] if t else [(1 - side) * 2, (1 - side) * 2 + 1]
        drain(outb.at[t, :, pl.ds(0, ROWS * len(owners))], cross_recv.at[t])

        @pl.when(is_gate)
        def _():
            for group in range(3):
                for owner in owners:
                    spot = place(txt_refs, group, owner)
                    remote(spot, spot, pass_send.at[t], cross_recv.at[t], dp(partner)).start()

    def total(gate):
        return remote(racc.at[3], racc.at[3], total_send.at[gate - 1], total_recv.at[0], dp(gate))

    def end_exchange(n):
        drain(rbuf.at[n, pl.ds(1, 7)], red_send.at[n])
        drain(rbuf.at[n, pl.ds(1, 7)], red_recv.at[n])

    @pl.when(jnp.logical_not(is_gate))
    def _():
        for n in range(3):
            end_exchange(n)
            value = racc[n]
            for i in range(1, 8):
                value = value + rbuf[n, i]
            racc[n + 1] = value
            if n < 2:
                start_exchange(n + 1)

        @pl.when(me != extra)
        def _():
            for gate in (1, 2):
                total(gate).start()

    pass_on(0)

    @pl.when(extra // 2 != side)
    def _():
        pass_on(1)

    @pl.when(is_gate)
    def _():
        end_exchange(0)
        drain(racc.at[3], total_recv.at[0])

    @pl.when(jnp.logical_and(jnp.logical_not(is_gate), me != extra))
    def _():
        for gate in (1, 2):
            total(gate).wait_send()

    value = racc[3]
    gain_out[...] = value[:, :HEAD_DIM] + value[:, HEAD_DIM:]

    def finish(t):
        drain(outb.at[t], kept.at[t])
        drain(outb.at[t, :, pl.ds(0, 2 * ROWS)], text_send.at[t])

    finish(0)
    drain(outb.at[0, :, pl.ds(0, 4 * ROWS)], out_recv.at[0])
    drain(inb.at[0, :, pl.ds(0, 3 * ROWS)], in_send.at[0])

    @pl.when(me == extra)
    def _():
        finish(1)

    @pl.when(me != extra)
    def _():
        drain(outb.at[0, :, pl.ds(0, ROWS)], out_recv.at[1])
        drain(inb.at[0, :, pl.ds(0, ROWS)], in_send.at[1])

    @pl.when(partner == extra)
    def _():
        drain(outb.at[0, :, pl.ds(0, ROWS)], out_recv.at[2])

    @pl.when(is_gate)
    def _():
        drain(outb.at[0, :, pl.ds(0, 2 * ROWS)], pass_send.at[0])

    @pl.when(jnp.logical_and(is_gate, extra // 2 != side))
    def _():
        drain(outb.at[0, :, pl.ds(0, ROWS)], pass_send.at[1])


def store_kernel(a, b, c, d, e, oa, ob, oc, od, oe, stage, small, read, write):
    pieces = [(c.at[k, 0], oc.at[k, 0]) for k in range(3)] + [(d.at[k, 0], od.at[k, 0]) for k in range(3)]
    pieces += [(a.at[0], oa.at[0]), (b.at[0], ob.at[0])]
    steps = [(src, stage.at[n], dst) for n, (src, dst) in enumerate(pieces)] + [(e, small, oe)]
    reads = [pltpu.make_async_copy(src, mid, read.at[n]) for n, (src, mid, dst) in enumerate(steps)]
    writes = [pltpu.make_async_copy(mid, dst, write.at[n]) for n, (src, mid, dst) in enumerate(steps)]
    for copy in reads:
        copy.start()
    for copy, onward in zip(reads, writes):
        copy.wait()
        onward.start()
    for copy in writes:
        copy.wait()


def store(results):
    anywhere = pl.BlockSpec(memory_space=pl.ANY)
    rows, width = results[0].shape[1:]
    return pl.pallas_call(
        store_kernel,
        out_shape=tuple(jax.ShapeDtypeStruct(r.shape, r.dtype) for r in results),
        in_specs=[anywhere] * 5,
        out_specs=(anywhere,) * 5,
        scratch_shapes=[
            pltpu.VMEM((8, rows, width), bf16),
            pltpu.VMEM(results[4].shape, f32),
            pltpu.SemaphoreType.DMA((9,)),
            pltpu.SemaphoreType.DMA((9,)),
        ],
        compiler_params=pltpu.CompilerParams(vmem_limit_bytes=63 << 20),
        name="store_results",
    )(*results)


def local(iq, ik, iv, tq, tk, tv, ig, tg, gains):
    rows, width = iq.shape[1], iq.shape[2]
    anywhere = pl.BlockSpec(memory_space=pltpu.HBM)
    vmem = pl.BlockSpec(memory_space=pltpu.VMEM)
    dma = pltpu.SemaphoreType.DMA
    out = jax.ShapeDtypeStruct((1, rows, width), bf16)
    grads = jax.ShapeDtypeStruct((3, 1, rows, width), bf16)
    tall = (BLOCKS * ROWS, LANES)
    wide = (LANES, BLOCKS * ROWS)
    return store(pl.pallas_call(
        kernel,
        out_shape=(out, out, grads, grads, jax.ShapeDtypeStruct(gains.shape, f32)),
        in_specs=[anywhere] * 8 + [vmem],
        out_specs=(anywhere,) * 4 + (vmem,),
        scratch_shapes=[
            pltpu.VMEM((2, 4, *tall), bf16),
            pltpu.VMEM((2, 4, *tall), bf16),
            pltpu.VMEM((2, *tall), f32),
            pltpu.VMEM(tall, bf16),
            pltpu.VMEM(tall, f32),
            pltpu.VMEM(tall, f32),
            pltpu.VMEM(wide, bf16),
            pltpu.VMEM(wide, bf16),
            pltpu.VMEM(tall, f32),
            pltpu.VMEM(tall, f32),
            pltpu.VMEM((4, 4, LANES), f32),
            pltpu.VMEM((3, 8, 4, LANES), f32),
            dma((2,)),
            dma((2, 2)),
            dma((2,)),
            dma((2,)),
            dma((3,)),
            dma((2,)),
            dma((2,)),
            dma((3,)),
            dma((3,)),
            dma((2,)),
            dma((1,)),
            pltpu.SemaphoreType.REGULAR((3,)),
        ],
        compiler_params=pltpu.CompilerParams(
            collective_id=0, has_side_effects=True, vmem_limit_bytes=63 << 20
        ),
        name="joint_attention",
    )(iq, ik, iv, tq, tk, tv, ig, tg, gains))


def solution(mesh):
    image, text = P("seq", "dp", "tensor"), P("seq", None, "tensor")
    in_specs = (image, image, image, text, text, text, image, text, P())
    out_specs = (image, text, P(None, "seq", "dp", "tensor"), P(None, "seq", None, "tensor"), P())
    return jax.shard_map(local, mesh=mesh, in_specs=in_specs, out_specs=out_specs, check_vma=False)
```

```python
import jax
import jax.numpy as jnp
from jax import lax
from jax.experimental import pallas as pl
from jax.experimental.pallas import tpu as pltpu
from jax.sharding import PartitionSpec as P

HEAD_DIM = 64
EPSILON = 1e-6
ROWS = 128
LANES = 128
BLOCKS = 5
TEXT = 4 * ROWS
LOG2E = 1.4426950408889634
MESH = pl.DeviceIdType.MESH
NT = (((1,), (1,)), ((), ()))
f32, bf16 = jnp.float32, jnp.bfloat16


def dot(a, b):
    return jnp.dot(a, b, preferred_element_type=f32)


def dot_nt(a, b):
    return lax.dot_general(a, b, NT, preferred_element_type=f32)


def first_head():
    return lax.broadcasted_iota(jnp.int32, (BLOCKS * ROWS, LANES), 1) < HEAD_DIM


def same_head():
    row = lax.broadcasted_iota(jnp.int32, (2 * LANES, LANES), 0)
    lane = lax.broadcasted_iota(jnp.int32, (2 * LANES, LANES), 1)
    return jnp.where(lax.rem(row, LANES) // HEAD_DIM == lane // HEAD_DIM, 1.0, 0.0).astype(bf16)


def identity():
    row = lax.broadcasted_iota(jnp.int32, (LANES, LANES), 0)
    lane = lax.broadcasted_iota(jnp.int32, (LANES, LANES), 1)
    return jnp.where(row == lane, 1.0, 0.0).astype(bf16)


def head_mean(z, same):
    high = z.astype(bf16)
    low = (z - high.astype(f32)).astype(bf16)
    return dot(jnp.concatenate([high, low], axis=1), same) * (1.0 / HEAD_DIM)


def norm(x, same):
    r = lax.rsqrt(head_mean(x * x, same) + EPSILON)
    return x * r, r


def norm_back(y, u, r, gain, same):
    w = y * gain
    return (r * (w - u * head_mean(w * u, same))).astype(bf16)


def by_head(x, first):
    zero = jnp.zeros_like(x)
    return jnp.concatenate([jnp.where(first, x, zero), jnp.where(first, zero, x)], axis=0)


def own_blocks(x):
    return jnp.concatenate([x[:HEAD_DIM, : BLOCKS * ROWS], x[HEAD_DIM:, BLOCKS * ROWS :]], axis=0)


def prepare_keys(ins, gain, nk, uk, rk, kt, vt):
    u, r = norm(ins[0].astype(f32), same_head())
    uk[...] = u
    rk[...] = r
    n = (u * gain).astype(bf16)
    nk[...] = n
    eye = identity()
    kt[...] = dot_nt(eye, n).astype(bf16)
    vt[...] = dot_nt(eye, ins[1]).astype(bf16)


def query_pass(ins, gain, nk, kt, vt, dk, dv, outs, send_output):
    same, first, eye = same_head(), first_head(), identity()
    u, r = norm(ins[2].astype(f32), same)
    q = by_head((u * gain).astype(bf16), first)
    cot = ins[3]
    g = by_head(cot, first)
    s = dot_nt(nk[...], q)
    e = jnp.exp2(s * (LOG2E * HEAD_DIM**-0.5))
    total = jnp.sum(e, axis=0, keepdims=True)
    p = e * (1.0 / total)
    pb = p.astype(bf16)
    out_t = own_blocks(dot(vt[...], pb)).astype(bf16)
    for b in range(BLOCKS):
        rows = slice(b * ROWS, (b + 1) * ROWS)
        outs[0, rows, :] = dot_nt(eye, out_t[:, rows]).astype(bf16)
    send_output()
    z = out_t.astype(f32) * dot_nt(eye, cot)
    delta = jnp.concatenate(
        [
            jnp.sum(z[:HEAD_DIM], axis=0, keepdims=True),
            jnp.sum(z[HEAD_DIM:], axis=0, keepdims=True),
        ],
        axis=1,
    )
    ds = (p * (dot_nt(ins[1], g) - delta)).astype(bf16)
    dk[...] = dot(ds, q)
    dv[...] = dot(pb, g)
    y = jnp.transpose(own_blocks(dot(kt[...], ds))) * HEAD_DIM**-0.5
    outs[1] = norm_back(y, u, r, gain, same)
    return y * u


def key_pass(gain, dk, dv, uk, rk, outs):
    y = dk[...] * HEAD_DIM**-0.5
    u, r = uk[...], rk[...]
    outs[2] = norm_back(y, u, r, gain, same_head())
    outs[3] = dv[...].astype(bf16)
    return y * u


def image_and_text(x):
    return [jnp.sum(x[:TEXT], axis=0, keepdims=True), jnp.sum(x[TEXT:], axis=0, keepdims=True)]


def kernel(
    iq, ik, iv, tq, tk, tv, ig, tg, gains_ref,
    img_out, txt_out, img_grads, txt_grads, gain_out,
    inb, outb, gain_rows, nk, uk, rk, kt, vt, dk, dv, racc, rbuf,
    in_send, in_recv, kept, text_send, out_recv, cross_recv, pass_send, red_send, red_recv, total_send, present,
):
    me = lax.axis_index("dp")
    seq = lax.axis_index("seq")
    tensor = lax.axis_index("tensor")
    core, z, x = lax.rem(seq, 2), lax.rem(seq // 2, 8), seq // 16
    y = tensor * 4 + me
    side = me // 2
    partner = me + 1 - 2 * lax.rem(me, 2)
    far_gate = 2 - side
    is_gate = jnp.logical_or(me == 1, me == 2)
    extra = 3 * jnp.where(tensor == 1, core, 1 - core)
    images = (ik, iv, iq, ig)
    texts = (tk, tv, tq, tg)

    def columns(owner):
        return pl.ds(pl.multiple_of(owner * LANES, LANES), LANES)

    def block(index):
        return pl.ds(pl.multiple_of(index * ROWS, ROWS), ROWS)

    def peer(i):
        return lax.rem(me + i, 4)

    def dp(index):
        return (index, seq, tensor)

    def remote(src, dst, send, recv, to):
        return pltpu.make_async_remote_copy(
            src_ref=src, dst_ref=dst, send_sem=send, recv_sem=recv, device_id=to, device_id_type=MESH
        )

    def drain(like, sem):
        pltpu.make_async_copy(like, like, sem).wait()

    def load(t):
        owner = me if t == 0 else 4
        for a in range(4):
            for refs, rows in ((texts, pl.ds(TEXT, ROWS)), (images, block(me))):
                pltpu.make_async_copy(
                    refs[a].at[0, :, columns(owner)], inb.at[t, a, rows], in_recv.at[t, a // 2]
                ).start()

    def along_y(k):
        return (lax.rem(k, 4), seq, k // 4)

    def along_x(k):
        return (me, (lax.rem(k, 4) * 8 + z) * 2 + k // 4, tensor)

    def along_z(who, k):
        return (who, (x * 8 + k) * 2 + core, tensor)

    source = 3 - extra
    is_source = me == source

    place_x = core * 4 + x
    rings = ((y, along_y), (place_x, along_x), (z, lambda k: along_z(me, k)))
    later = (4 * (1 - tensor), 7 - place_x, (7 - z) * jnp.where(is_source, 3, 1))
    barrier = pltpu.get_barrier_semaphore()

    def greet(sem, to):
        pl.semaphore_signal(sem, inc=1, device_id=to, device_id_type=MESH)

    for i in (1, 2, 3):
        greet(barrier, dp(peer(i)))

    def each_pair(act, want_later):
        @pl.when(tensor == (0 if want_later else 1))
        def _():
            for k in range(4):
                act(0, (k, seq, 1 - tensor))

        @pl.when(jnp.logical_not(is_gate))
        def _():
            for n in (1, 2):
                mine, member = rings[n]
                for k in range(8):
                    ahead = mine < k if want_later else mine > k

                    @pl.when(ahead)
                    def _():
                        act(n, member(k))

        for k in range(8):
            ahead = z < k if want_later else z > k

            @pl.when(jnp.logical_and(is_gate, ahead))
            def _():
                act(2, along_z(source, k))

            if want_later:

                @pl.when(jnp.logical_and(is_source, ahead))
                def _():
                    for gate in (1, 2):
                        act(2, along_z(gate, k))

    each_pair(lambda n, to: greet(barrier, to), True)
    load(0)

    @pl.when(me == extra)
    def _():
        load(1)

    pl.semaphore_wait(barrier, 3 + 4 * tensor + jnp.where(is_gate, z, place_x + z * jnp.where(is_source, 3, 1)))

    def hand(a, i):
        to = peer(i)
        remote(
            images[a].at[0, :, columns(to)], inb.at[0, a, block(me)],
            in_send.at[0], in_recv.at[0, a // 2], dp(to),
        ).start()

    for pair in ((0, 1), (2, 3)):
        for i in (2, 3, 1):
            for a in pair:
                hand(a, i)

    @pl.when(me != extra)
    def _():
        for a in range(4):
            remote(
                images[a].at[0, :, columns(4)], inb.at[1, a, block(me)],
                in_send.at[1], in_recv.at[1, a // 2], dp(extra),
            ).start()

    each_pair(lambda n, to: greet(present.at[n], to), False)

    def result(t, group, rows):
        return outb.at[t, pl.ds(2, 2), rows] if group == 2 else outb.at[t, group, rows]

    def place(refs, group, owner):
        if group == 0:
            return refs[0].at[0, :, columns(owner)]
        if group == 1:
            return refs[1].at[0, 0, :, columns(owner)]
        return refs[1].at[pl.ds(1, 2), 0, :, columns(owner)]

    img_refs, txt_refs = (img_out, img_grads), (txt_out, txt_grads)

    def owner_of(t):
        return jnp.where(t == 0, me, 4)

    def send_text(t, groups):
        for group in groups:
            rows = result(t, group, pl.ds(TEXT, ROWS))
            spot = place(txt_refs, group, owner_of(t))
            remote(rows, spot, text_send.at[t], cross_recv.at[t], dp(far_gate)).start()
            remote(rows, spot, text_send.at[t], out_recv.at[2 * t], dp(partner)).start()
            pltpu.make_async_copy(rows, spot, kept.at[t]).start()

    def send_images(t, groups):
        for group in groups:
            spot = place(img_refs, group, owner_of(t))
            for i in (2, 3, 1):
                to = peer(i)
                remote(result(t, group, block(to)), spot, kept.at[t], out_recv.at[t], dp(to)).start()
            pltpu.make_async_copy(result(t, group, block(me)), spot, kept.at[t]).start()

    def start_exchange(n):
        @pl.when(later[n] > 0)
        def _():
            pl.semaphore_wait(present.at[n], later[n])

        mine, member = rings[n]
        for i in range(1, 8):
            remote(
                racc.at[n], rbuf.at[n, i], red_send.at[n], red_recv.at[n], member(lax.rem(mine + i, 8))
            ).start()

    pairs = jnp.concatenate([gains_ref[...]] * 2, axis=1)
    is_text = lax.broadcasted_iota(jnp.int32, (BLOCKS * ROWS, LANES), 0) >= TEXT
    for k in range(2):
        gain_rows[k] = jnp.where(is_text, pairs[k + 2 : k + 3], pairs[k : k + 1])
    racc[0] = jnp.zeros((4, LANES), f32)

    def do_tile(t, carry):
        ins, outs = inb.at[t], outb.at[t]

        def send_output():
            @pl.when(jnp.logical_and(t == 0, me != extra))
            def _():
                send_text(0, (0,))

        drain(inb.at[t, pl.ds(0, 2)], in_recv.at[t, 0])
        prepare_keys(ins, gain_rows[1], nk, uk, rk, kt, vt)
        drain(inb.at[t, pl.ds(2, 2)], in_recv.at[t, 1])
        query = image_and_text(query_pass(ins, gain_rows[0], nk, kt, vt, dk, dv, outs, send_output))
        key = image_and_text(key_pass(gain_rows[1], dk, dv, uk, rk, outs))
        racc[0] += jnp.concatenate([query[0], key[0], query[1], key[1]], axis=0)

        @pl.when(t == 0)
        def _():
            @pl.when(me != extra)
            def _():
                start_exchange(0)

            @pl.when(me != extra)
            def _():
                send_text(0, (1, 2))
                send_images(0, (0, 1, 2))

        @pl.when(t == 1)
        def _():
            start_exchange(0)
            send_text(0, (0, 1, 2))
            send_text(1, (0, 1, 2))
            send_images(0, (0, 1, 2))
            send_images(1, (0, 1, 2))

        return carry

    lax.fori_loop(0, jnp.where(me == extra, 2, 1), do_tile, 0)

    def pass_on(t):
        owners = [4] if t else [(1 - side) * 2, (1 - side) * 2 + 1]
        drain(outb.at[t, :, pl.ds(0, ROWS * len(owners))], cross_recv.at[t])

        @pl.when(is_gate)
        def _():
            for group in range(3):
                for owner in owners:
                    spot = place(txt_refs, group, owner)
                    remote(spot, spot, pass_send.at[t], cross_recv.at[t], dp(partner)).start()

    def end_exchange(n):
        drain(rbuf.at[n, pl.ds(1, 7)], red_send.at[n])
        drain(rbuf.at[n, pl.ds(1, 7)], red_recv.at[n])

    @pl.when(jnp.logical_not(is_gate))
    def _():
        for n in range(3):
            end_exchange(n)
            value = racc[n]
            for i in range(1, 8):
                value = value + rbuf[n, i]
            racc[n + 1] = value
            if n < 2:
                start_exchange(n + 1)
            if n == 1:

                @pl.when(is_source)
                def _():
                    for gate in (1, 2):
                        for i in range(8):
                            remote(
                                racc.at[2], rbuf.at[2, i], total_send.at[0], red_recv.at[2],
                                along_z(gate, lax.rem(z + i, 8)),
                            ).start()


    pass_on(0)

    @pl.when(extra // 2 != side)
    def _():
        pass_on(1)

    @pl.when(is_gate)
    def _():
        end_exchange(0)
        drain(rbuf.at[2], red_recv.at[2])
        value = rbuf[2, 0]
        for i in range(1, 8):
            value = value + rbuf[2, i]
        racc[3] = value

    @pl.when(is_source)
    def _():
        drain(rbuf.at[pl.ds(0, 2)], total_send.at[0])

    value = racc[3]
    gain_out[...] = value[:, :HEAD_DIM] + value[:, HEAD_DIM:]

    def finish(t):
        drain(outb.at[t], kept.at[t])
        drain(outb.at[t, :, pl.ds(0, 2 * ROWS)], text_send.at[t])

    finish(0)
    drain(outb.at[0, :, pl.ds(0, 4 * ROWS)], out_recv.at[0])
    drain(inb.at[0, :, pl.ds(0, 3 * ROWS)], in_send.at[0])

    @pl.when(me == extra)
    def _():
        finish(1)

    @pl.when(me != extra)
    def _():
        drain(outb.at[0, :, pl.ds(0, ROWS)], out_recv.at[1])
        drain(inb.at[0, :, pl.ds(0, ROWS)], in_send.at[1])

    @pl.when(partner == extra)
    def _():
        drain(outb.at[0, :, pl.ds(0, ROWS)], out_recv.at[2])

    @pl.when(is_gate)
    def _():
        drain(outb.at[0, :, pl.ds(0, 2 * ROWS)], pass_send.at[0])

    @pl.when(jnp.logical_and(is_gate, extra // 2 != side))
    def _():
        drain(outb.at[0, :, pl.ds(0, ROWS)], pass_send.at[1])


def store_kernel(a, b, c, d, e, oa, ob, oc, od, oe, stage, small, read, write):
    pieces = [(c.at[k, 0], oc.at[k, 0]) for k in range(3)] + [(d.at[k, 0], od.at[k, 0]) for k in range(3)]
    pieces += [(a.at[0], oa.at[0]), (b.at[0], ob.at[0])]
    steps = [(src, stage.at[n], dst) for n, (src, dst) in enumerate(pieces)] + [(e, small, oe)]
    reads = [pltpu.make_async_copy(src, mid, read.at[n]) for n, (src, mid, dst) in enumerate(steps)]
    writes = [pltpu.make_async_copy(mid, dst, write.at[n]) for n, (src, mid, dst) in enumerate(steps)]
    for copy in reads:
        copy.start()
    for copy, onward in zip(reads, writes):
        copy.wait()
        onward.start()
    for copy in writes:
        copy.wait()


def store(results):
    anywhere = pl.BlockSpec(memory_space=pl.ANY)
    rows, width = results[0].shape[1:]
    return pl.pallas_call(
        store_kernel,
        out_shape=tuple(jax.ShapeDtypeStruct(r.shape, r.dtype) for r in results),
        in_specs=[anywhere] * 5,
        out_specs=(anywhere,) * 5,
        scratch_shapes=[
            pltpu.VMEM((8, rows, width), bf16),
            pltpu.VMEM(results[4].shape, f32),
            pltpu.SemaphoreType.DMA((9,)),
            pltpu.SemaphoreType.DMA((9,)),
        ],
        compiler_params=pltpu.CompilerParams(vmem_limit_bytes=63 << 20),
        name="store_results",
    )(*results)


def local(iq, ik, iv, tq, tk, tv, ig, tg, gains):
    rows, width = iq.shape[1], iq.shape[2]
    anywhere = pl.BlockSpec(memory_space=pltpu.HBM)
    vmem = pl.BlockSpec(memory_space=pltpu.VMEM)
    dma = pltpu.SemaphoreType.DMA
    out = jax.ShapeDtypeStruct((1, rows, width), bf16)
    grads = jax.ShapeDtypeStruct((3, 1, rows, width), bf16)
    tall = (BLOCKS * ROWS, LANES)
    wide = (LANES, BLOCKS * ROWS)
    return store(pl.pallas_call(
        kernel,
        out_shape=(out, out, grads, grads, jax.ShapeDtypeStruct(gains.shape, f32)),
        in_specs=[anywhere] * 8 + [vmem],
        out_specs=(anywhere,) * 4 + (vmem,),
        scratch_shapes=[
            pltpu.VMEM((2, 4, *tall), bf16),
            pltpu.VMEM((2, 4, *tall), bf16),
            pltpu.VMEM((2, *tall), f32),
            pltpu.VMEM(tall, bf16),
            pltpu.VMEM(tall, f32),
            pltpu.VMEM(tall, f32),
            pltpu.VMEM(wide, bf16),
            pltpu.VMEM(wide, bf16),
            pltpu.VMEM(tall, f32),
            pltpu.VMEM(tall, f32),
            pltpu.VMEM((4, 4, LANES), f32),
            pltpu.VMEM((3, 8, 4, LANES), f32),
            dma((2,)),
            dma((2, 2)),
            dma((2,)),
            dma((2,)),
            dma((3,)),
            dma((2,)),
            dma((2,)),
            dma((3,)),
            dma((3,)),
            dma((1,)),
            pltpu.SemaphoreType.REGULAR((3,)),
        ],
        compiler_params=pltpu.CompilerParams(
            collective_id=0, has_side_effects=True, vmem_limit_bytes=63 << 20
        ),
        name="joint_attention",
    )(iq, ik, iv, tq, tk, tv, ig, tg, gains))


def solution(mesh):
    image, text = P("seq", "dp", "tensor"), P("seq", None, "tensor")
    in_specs = (image, image, image, text, text, text, image, text, P())
    out_specs = (image, text, P(None, "seq", "dp", "tensor"), P(None, "seq", None, "tensor"), P())
    return jax.shard_map(local, mesh=mesh, in_specs=in_specs, out_specs=out_specs, check_vma=False)
```
